1024 devices in a mesh: tm: 256 (over y, x_lo, z), mp: 4 (over x_hi, core).
Axes of the slice: x: 8 (x_hi: 2, x_lo: 4; x = x_hi * 4 + x_lo), y: 8, z: 8, core: 2. Of those that a mesh axis runs over, the one named last changes fastest.
Arguments:
- frames: bfloat16 [65536, 1536], P('tm', 'mp'), may hold values from -6 to 6
- ffn_gain: float32 [1536], replicated, may hold values from 0.2 to 5
- w_up: bfloat16 [1536, 3072], P(None, 'mp'), may hold values from -0.15625 to 0.15625
- w_down: bfloat16 [3072, 1536], P('mp'), may hold values from -0.21875 to 0.21875
- ln_gain: float32 [1536], replicated, may hold values from 0.25 to 1.75
- w_qkv: bfloat16 [1536, 3, 1536], P(None, None, 'mp')
- w_out: bfloat16 [1536, 1536], P('mp'), may hold values from -0.3125 to 0.3125
- conv_kernel: float32 [31, 1536], P(None, 'mp'), may hold values from -2 to 2
- left_groups: int32 [256], P('tm'), may hold values from 0 to 3, as said below
- start_offset: int32 [256], P('tm'), may hold values from 0 to 127
Outputs:
- block_out: bfloat16 [65536, 1536], P('tm', 'mp')
The draws below stay inside these ranges and needn't reach their ends.
Inputs may be any that keep to these rules, and one draw needn't show every extreme that they name: left_groups[c] is at most the number of groups of c's recording that lie before c: context never crosses a recording.
All inputs are finite; a program needn't handle non-finite values.
Results may differ from the reference program's by a relative error of at most 0.04.
Values may be sent and summed in bfloat16 or wider, within the bound.
A program may use at most 64 MiB of HBM per device.

```python
import math
import jax
import jax.numpy as jnp
from jax import lax

D = 1536
FF = 3072
HEADS = 24
HEAD_DIM = 64
KERNEL = 31
LEFT = 3
TOK_DEV = 256
REC_SHARDS = 8
TOKENS = 65536
N_TM = 256
N_MP = 4


def draw_w_qkv(key, part):
    base = jax.random.normal(key, (D, 3, D), jnp.float32) * D ** (-0.5)
    query_part = base[:, 0, :] * 1.6
    key_part = base[:, 1, :] * 1.6
    return jnp.stack([query_part, key_part, base[:, 2, :]], axis=1).astype(jnp.bfloat16)


def draw_left_groups(key, part):
    group = jnp.arange(N_TM, dtype=jnp.int32)
    within = jnp.where(group < REC_SHARDS // 2, group, (group - REC_SHARDS // 2) % REC_SHARDS)
    picked = jax.random.randint(key, (N_TM,), 1, LEFT + 1, dtype=jnp.int32)
    picked = jnp.minimum(picked, within)
    return picked.at[REC_SHARDS // 2 + LEFT].set(LEFT)


def draw_start_offset(key, part):
    picked = jax.random.randint(key, (N_TM,), 0, TOK_DEV // 2, dtype=jnp.int32)
    picked = picked.at[0].set(TOK_DEV // 2 - 1)
    return picked.at[1].set(0)


def block_levels(rng, shape, cuts, least, top_value):
    loudness, own = 1.0, jax.random.fold_in(rng, 6)
    for axis_at, shards_of in cuts:
        heights = jnp.exp(jax.random.uniform(jax.random.fold_in(own, axis_at), (shards_of,), jnp.float32, least / len(cuts), top_value / len(cuts)))
        loudness = loudness * jnp.repeat(heights, shape[axis_at] // shards_of).reshape([-1 if axis == axis_at else 1 for axis in range(len(shape))])
    return loudness


def gaussian(own_key, shape, scale, reach, pieces=(), held_as=jnp.bfloat16):
    drawn = scale * jax.random.normal(own_key, shape, jnp.float32)
    if pieces:
        drawn = drawn * block_levels(own_key, shape, pieces, -0.22, 0.18)
    return jnp.clip(drawn, -reach, reach).astype(held_as)


def setup_inputs(seed: int = 0) -> dict:
    splits = jax.random.split(jax.random.key(seed), 11)
    return {
        "frames": gaussian(splits[0], (TOKENS, D), 1.0, 6.0, ((0, 256), (1, 4))),
        "ffn_gain": jnp.clip(jnp.exp(jax.random.uniform(splits[1], (D,), jnp.float32, math.log(0.2), math.log(5.0))), 0.2, 5.0),
        "w_up": gaussian(splits[2], (D, FF), D ** -0.5, 0.15625, ((1, 4),)),
        "w_down": gaussian(splits[3], (FF, D), (FF // 4) ** -0.5, 0.21875, ((0, 4),)),
        "ln_gain": jnp.clip(1.0 + 0.15 * jax.random.normal(splits[4], (D,), jnp.float32), 0.25, 1.75),
        "w_qkv": draw_w_qkv(jax.random.fold_in(splits[10], 71), 0),
        "w_out": gaussian(splits[6], (D, D), (D // 4) ** -0.5, 0.3125, ((0, 4),)),
        "conv_kernel": gaussian(splits[7], (KERNEL, D), 0.35, 2.0, ((1, 4),), jnp.float32),
        "left_groups": draw_left_groups(jax.random.fold_in(splits[10], 71), 0),
        "start_offset": draw_start_offset(jax.random.fold_in(splits[10], 71), 0),
    }


def layer_norm(values_in, gain):
    widened = values_in.astype(jnp.float32)
    center = lax.optimization_barrier(jnp.mean(widened, axis=-1, keepdims=True))
    spread = lax.optimization_barrier(jnp.mean((widened - center) ** 2, axis=-1, keepdims=True))
    return ((widened - center) * lax.rsqrt(spread + 1e-05) * gain).astype(jnp.bfloat16)

def reference(frames, ffn_gain, w_up, w_down, ln_gain, w_qkv, w_out, conv_kernel, left_groups, start_offset):
    ffn_normed = layer_norm(frames, ffn_gain)
    ffn_hidden = jax.nn.silu(jnp.dot(ffn_normed, w_up, preferred_element_type=jnp.float32)).astype(jnp.bfloat16)
    block = FF // N_MP
    ffn_total = jnp.zeros((TOKENS, D), jnp.float32)
    for block_index in range(N_MP):
        piece = jnp.dot(ffn_hidden[:, block_index * block:(block_index + 1) * block], w_down[block_index * block:(block_index + 1) * block], preferred_element_type=jnp.float32)
        ffn_total = ffn_total + lax.optimization_barrier(piece.astype(jnp.bfloat16)).astype(jnp.float32)
    ffn_mid = (frames.astype(jnp.float32) + 0.5 * ffn_total).astype(jnp.bfloat16)
    normed = layer_norm(ffn_mid, ln_gain)
    projected = jnp.dot(normed, w_qkv.reshape(D, 3 * D), preferred_element_type=jnp.float32).astype(jnp.bfloat16)
    queries = projected[:, :D].reshape(N_TM, TOK_DEV, HEADS, HEAD_DIM)
    key_value = projected[:, D:].reshape(N_TM, TOK_DEV, 2 * D)
    keys_padded = jnp.concatenate([jnp.zeros((LEFT, TOK_DEV, 2 * D), jnp.bfloat16), key_value], axis=0)
    scale = HEAD_DIM ** (-0.5)
    key_index = jnp.arange((LEFT + 1) * TOK_DEV, dtype=jnp.int32)
    distance = LEFT - key_index // TOK_DEV
    position = key_index % TOK_DEV

    def one_group(group):
        group = group.astype(jnp.int32)
        window = lax.dynamic_slice_in_dim(keys_padded, group, LEFT + 1, 0).reshape((LEFT + 1) * TOK_DEV, 2 * D)
        keys = window[:, :D].reshape(-1, HEADS, HEAD_DIM).astype(jnp.float32)
        values = window[:, D:].reshape(-1, HEADS, HEAD_DIM).astype(jnp.float32)
        left_count = left_groups[group]
        offset = start_offset[group]
        visible = (distance < left_count) | (distance == left_count) & ((left_count == 0) | (position >= offset))
        scores = jnp.einsum('thd,jhd->htj', queries[group].astype(jnp.float32), keys) * scale
        scores = jnp.where(visible[None, None, :], scores, -jnp.inf)
        highest = lax.optimization_barrier(jnp.max(scores, axis=-1, keepdims=True))
        expo = jnp.where(visible[None, None, :], jnp.exp(scores - highest), 0.0)
        attn_weights = (expo / lax.optimization_barrier(jnp.sum(expo, axis=-1, keepdims=True))).astype(jnp.bfloat16)
        context = jnp.einsum('htj,jhd->thd', attn_weights.astype(jnp.float32), values)
        return context.astype(jnp.bfloat16).reshape(TOK_DEV, D)
    context = lax.map(one_group, jnp.arange(N_TM, dtype=jnp.int32)).reshape(TOKENS, D)
    attn_out = jnp.dot(context, w_out, preferred_element_type=jnp.float32)
    mid = (ffn_mid.astype(jnp.float32) + attn_out).astype(jnp.bfloat16)
    half = (KERNEL - 1) // 2
    lead = REC_SHARDS // 2 * TOK_DEV
    extended = jnp.pad(mid.astype(jnp.float32), ((lead, lead), (0, 0)))
    records = extended.reshape(N_TM // REC_SHARDS + 1, REC_SHARDS * TOK_DEV, D)
    padded = jnp.pad(records, ((0, 0), (half, half), (0, 0)))
    accumulated = jnp.zeros_like(records)
    for tap_index in range(KERNEL):
        accumulated = accumulated + conv_kernel[tap_index] * padded[:, tap_index:tap_index + REC_SHARDS * TOK_DEV, :]
    result = (records + jax.nn.silu(accumulated)).reshape(-1, D)[lead:lead + TOKENS]
    return result.astype(jnp.bfloat16)
```

```python
import functools

import jax
import jax.numpy as jnp
from jax import lax
from jax.experimental import pallas as pl
from jax.experimental.pallas import tpu as pltpu
from jax.sharding import PartitionSpec as P

HEAD_DIM = 64
KERNEL = 31
LEFT = 3
REC_SHARDS = 8
CHUNKS = 2
LANES = 128
HALO = 16
HIDDEN_STEP = 256
NEVER = -1e30
F32 = jnp.float32
BF16 = jnp.bfloat16


def layer_norm(values_in, gain):
    widened = values_in.astype(F32)
    center = jnp.mean(widened, axis=-1, keepdims=True)
    shifted = widened - center
    spread = jnp.mean(shifted * shifted, axis=-1, keepdims=True)
    return (shifted * lax.rsqrt(spread + 1e-05) * gain).astype(BF16)


def dot(a, b, dims=((1,), (0,))):
    return lax.dot_general(a, b, (dims, ((), ())), preferred_element_type=F32)


def block_kernel(
    left_ref, offset_ref, frames, ffn_gain, w_up, w_down, ln_gain, w_qkv, w_out, taps, out,
    whole, up_v, down_v, qkv_v, out_v, hidden, normed, partial, partial_in, chip_out, chip_in,
    ffn_mid, queries, kv, scores, context, proj, proj_in, cross_out, cross_in, padded,
    edge_out, edge_in, local_sem, send_sem, recv_sem,
):
    rows, width = frames.shape
    d_model = whole.shape[1]
    size = rows // CHUNKS
    half = size // 2
    groups = lax.axis_size("tm")
    group = lax.axis_index("tm")
    me = lax.axis_index("mp")
    core = lax.rem(me, 2)
    side = me // 2
    sibling = me + 1 - 2 * core
    partner = lax.rem(me + 2, 4)
    following = lax.rem(group + 1, groups)
    previous = lax.rem(group + groups - 1, groups)

    loads = []
    for i, (src, dst) in enumerate(
        ((w_up, up_v), (w_down, down_v), (w_qkv, qkv_v), (w_out, out_v))
    ):
        loads.append(pltpu.make_async_copy(src, dst, local_sem.at[i]))
    own_cols = pl.ds(pl.multiple_of(me * width, LANES), width)
    own_frames = pltpu.make_async_copy(frames, whole.at[:, own_cols], local_sem.at[4])
    own_frames.start()
    for load in loads:
        load.start()

    barrier = pltpu.get_barrier_semaphore()
    for target in ({"mp": sibling}, {"mp": partner}, {"tm": following}, {"tm": previous}):
        pl.semaphore_signal(
            barrier, inc=1, device_id=target, device_id_type=pl.DeviceIdType.MESH
        )
    pl.semaphore_wait(barrier, 4)

    copies = []

    def send(src, dst, target):
        i = len(copies)
        copy = pltpu.make_async_remote_copy(
            src_ref=src, dst_ref=dst, send_sem=send_sem.at[i], recv_sem=recv_sem.at[i],
            device_id=target, device_id_type=pl.DeviceIdType.MESH,
        )
        copies.append(copy)
        copy.start()
        return copy

    def span(r):
        return pl.ds(r * size, size)

    def shared(r):
        return pl.ds(pl.multiple_of(r * size + core * half, half), half)

    to_partner, to_sibling = [], []
    for r in range(CHUNKS):
        to_partner.append(
            send(frames.at[span(r), :], whole.at[span(r), own_cols], {"mp": partner})
        )
        to_sibling.append(
            send(frames.at[span(r), :], whole.at[span(r), own_cols], {"mp": sibling})
        )
    own_frames.wait()

    partner_cols = pl.ds(pl.multiple_of(partner * width, LANES), width)
    crossing = []
    for r in range(CHUNKS):
        to_partner[r].wait_recv()
        passed_on = send(
            whole.at[span(r), partner_cols], whole.at[span(r), partner_cols], {"mp": sibling}
        )
        to_sibling[r].wait_recv()
        passed_on.wait_recv()
        normed[...] = layer_norm(whole[span(r), :], ffn_gain[...])
        if r == 0:
            loads[0].wait()

        @pl.loop(0, up_v.shape[1] // HIDDEN_STEP)
        def _(j):
            cols = pl.ds(pl.multiple_of(j * HIDDEN_STEP, HIDDEN_STEP), HIDDEN_STEP)
            v = dot(normed[...], up_v[:, cols])
            hidden[:, cols] = (v / (1.0 + jnp.exp(-v))).astype(BF16)

        if r == 0:
            loads[1].wait()

        @pl.loop(0, d_model // HIDDEN_STEP)
        def _(j):
            cols = pl.ds(pl.multiple_of(j * HIDDEN_STEP, HIDDEN_STEP), HIDDEN_STEP)
            partial[r, :, cols] = dot(hidden[...], down_v[:, cols]).astype(BF16)

        mine = pl.ds(pl.multiple_of(core * half, half), half)
        theirs = pl.ds(pl.multiple_of((1 - core) * half, half), half)
        swap = send(partial.at[r, theirs, :], partial_in.at[r], {"mp": sibling})
        swap.wait_recv()
        chip_out[r] = (partial[r, mine, :].astype(F32) + partial_in[r].astype(F32)).astype(BF16)
        crossing.append(send(chip_out.at[r], chip_in.at[r], {"mp": partner}))

    hops = {}

    def hop(h, r):
        if h > 1:
            hops[h - 1, r].wait_recv()
        hops[h, r] = send(kv.at[h - 1, span(r), :], kv.at[h, span(r), :], {"tm": following})

    for r in range(CHUNKS):
        crossing[r].wait_recv()
        total = chip_out[r].astype(F32) + chip_in[r].astype(F32)
        ffn_mid[shared(r), :] = (whole[shared(r), :].astype(F32) + 0.5 * total).astype(BF16)
        joined = send(ffn_mid.at[shared(r), :], ffn_mid.at[shared(r), :], {"mp": sibling})
        joined.wait_recv()
        normed[...] = layer_norm(ffn_mid[span(r), :], ln_gain[...])
        if r == 0:
            loads[2].wait()
        for c in (1, 2):
            cols = slice(c * width, (c + 1) * width)
            kv[0, span(r), slice((c - 1) * width, c * width)] = dot(
                normed[...], qkv_v[:, cols]
            ).astype(BF16)
        hop(1, r)
        queries[span(r), :] = (
            dot(normed[...], qkv_v[:, 0:width]).astype(BF16) * (HEAD_DIM ** -0.5)
        ).astype(BF16)
        for h in range(2, LEFT + 1):
            if r - h + 1 >= 0:
                hop(h, r - h + 1)

    left = left_ref[0]
    offset = offset_ref[0]
    position = lax.broadcasted_iota(jnp.int32, (rows, rows), 1)
    upper = lax.broadcasted_iota(jnp.int32, (rows, LANES), 1) >= HEAD_DIM

    def score(d):
        if d > 0:
            first = jnp.where(d < left, 0, jnp.where(d == left, offset, rows))
            shown = position >= first

        @pl.loop(0, width // LANES)
        def _(p):
            cols = pl.ds(pl.multiple_of(p * LANES, LANES), LANES)
            pair = queries[:, cols]
            keys = kv[d, :, cols]
            for odd in range(2):
                picked = jnp.where(upper if odd else jnp.logical_not(upper), pair, 0)
                s = dot(picked, keys, ((1,), (1,)))
                if d > 0:
                    s = jnp.where(shown, s, NEVER)
                scores[2 * p + odd, :, d * rows : (d + 1) * rows] = s

    todo = [(h, r) for r in range(CHUNKS) for h in range(2, LEFT + 1) if r + h - 1 >= CHUNKS]
    todo.sort(key=lambda item: (item[0] + item[1], item[1]))
    late = [item for item in todo if item[0] + item[1] <= CHUNKS]
    for item in late:
        hop(*item)
    score(0)
    rest = [item for item in todo if item not in late]
    for d in range(1, LEFT + 1):
        for item in [i for i in rest if i[0] + i[1] == CHUNKS + d]:
            hop(*item)
        for r in range(CHUNKS):
            if (d + 1, r) not in hops:
                hops[d, r].wait_recv()
        score(d)

    lower = lax.broadcasted_iota(jnp.int32, (size, LANES), 1) < HEAD_DIM
    swaps, outgoing = [], []
    loads[3].wait()
    for r in range(CHUNKS):

        @pl.loop(0, width // LANES)
        def _(p):
            cols = pl.ds(pl.multiple_of(p * LANES, LANES), LANES)
            val_cols = pl.ds(pl.multiple_of(width + p * LANES, LANES), LANES)
            found = []
            for odd in range(2):
                s = scores[2 * p + odd, span(r), :]
                e = jnp.exp(s - jnp.max(s, axis=-1, keepdims=True))
                norm = jnp.sum(e, axis=-1, keepdims=True)
                e = e.astype(BF16)
                acc = None
                for d in range(LEFT + 1):
                    term = dot(e[:, d * rows : (d + 1) * rows], kv[d, :, val_cols])
                    acc = term if acc is None else acc + term
                found.append(acc / norm)
            context[span(r), cols] = jnp.where(lower, found[0], found[1]).astype(BF16)

        for k in range(4):
            proj[r, (k % 2) * 2 + k // 2] = dot(
                context[span(r), :], out_v[:, k * width : (k + 1) * width]
            ).astype(BF16)
        swap = send(
            proj.at[r, pl.ds((1 - core) * 2, 2)], proj_in.at[r], {"mp": sibling}
        )
        swap.wait_recv()
        far = 1 - side
        cross_out[r] = (
            proj[r, core * 2 + far].astype(F32) + proj_in[r, far].astype(F32)
        ).astype(BF16)
        outgoing.append(send(cross_out.at[r], cross_in.at[r], {"mp": partner}))

    for r in range(CHUNKS):
        own = (
            ffn_mid[span(r), own_cols].astype(F32)
            + proj[r, core * 2 + side].astype(F32)
            + proj_in[r, side].astype(F32)
        )
        outgoing[r].wait_recv()
        mid = (own + cross_in[r].astype(F32)).astype(BF16)
        padded[HALO + r * size : HALO + (r + 1) * size, :] = mid.astype(F32)
        if r == 0:
            edge_out[0] = mid[:HALO]
            back = send(edge_out.at[0], edge_in.at[0], {"tm": previous})
        if r == CHUNKS - 1:
            edge_out[1] = mid[size - HALO :]
            ahead = send(edge_out.at[1], edge_in.at[1], {"tm": following})
    place = lax.rem(group, REC_SHARDS)
    starts = jnp.logical_or(place == REC_SHARDS // 2, group == 0)
    ends = jnp.logical_or(place == REC_SHARDS // 2 - 1, group == groups - 1)
    back.wait_recv()
    padded[HALO + rows :, :] = edge_in[0].astype(F32) * jnp.where(ends, 0.0, 1.0)
    ahead.wait_recv()
    padded[:HALO, :] = edge_in[1].astype(F32) * jnp.where(starts, 0.0, 1.0)

    block = min(64, rows)
    for c in range(width // LANES):
        cols = slice(c * LANES, (c + 1) * LANES)

        @pl.loop(0, rows // block)
        def _(i):
            base = pl.multiple_of(i * block, block)
            near = padded[pl.ds(base, block + 2 * HALO), cols]
            total = jnp.zeros((block, LANES), F32)
            for shift in range(8):
                moved = near
                if shift:
                    moved = pltpu.roll(near, block + 2 * HALO - shift, 0)
                for up in range(0, 2 * HALO, 8):
                    tap = up + shift - 1
                    if 0 <= tap < KERNEL:
                        total = total + taps[tap : tap + 1, cols] * moved[up : up + block]
            mid = near[HALO : HALO + block]
            out[pl.ds(base, block), cols] = (
                mid + total / (1.0 + jnp.exp(-total))
            ).astype(BF16)

    for copy in copies:
        copy.wait_send()


def body(
    frames, ffn_gain, w_up, w_down, ln_gain, w_qkv, w_out, conv_kernel, left_groups, start_offset
):
    rows, width = frames.shape
    d_model = w_up.shape[0]
    hidden = w_up.shape[1]
    size = rows // CHUNKS
    pairs = CHUNKS * (3 + 1 + 1 + 1 + LEFT + 1 + 1) + 2
    anywhere = pl.BlockSpec(memory_space=pl.ANY)
    in_vmem = pl.BlockSpec(memory_space=pltpu.VMEM)
    in_smem = pl.BlockSpec(memory_space=pltpu.SMEM)
    return pl.pallas_call(
        block_kernel,
        out_shape=jax.ShapeDtypeStruct((rows, width), BF16),
        in_specs=[
            in_smem, in_smem, anywhere, in_vmem, anywhere, anywhere, in_vmem, anywhere, anywhere,
            in_vmem,
        ],
        out_specs=in_vmem,
        scratch_shapes=[
            pltpu.VMEM((rows, d_model), BF16),
            pltpu.VMEM(w_up.shape, BF16),
            pltpu.VMEM(w_down.shape, BF16),
            pltpu.VMEM((d_model, 3 * width), BF16),
            pltpu.VMEM(w_out.shape, BF16),
            pltpu.VMEM((size, hidden), BF16),
            pltpu.VMEM((size, d_model), BF16),
            pltpu.VMEM((CHUNKS, size, d_model), BF16),
            pltpu.VMEM((CHUNKS, size // 2, d_model), BF16),
            pltpu.VMEM((CHUNKS, size // 2, d_model), BF16),
            pltpu.VMEM((CHUNKS, size // 2, d_model), BF16),
            pltpu.VMEM((rows, d_model), BF16),
            pltpu.VMEM((rows, width), BF16),
            pltpu.VMEM((LEFT + 1, rows, 2 * width), BF16),
            pltpu.VMEM((width // HEAD_DIM, rows, (LEFT + 1) * rows), F32),
            pltpu.VMEM((rows, width), BF16),
            pltpu.VMEM((CHUNKS, 4, size, width), BF16),
            pltpu.VMEM((CHUNKS, 2, size, width), BF16),
            pltpu.VMEM((CHUNKS, size, width), BF16),
            pltpu.VMEM((CHUNKS, size, width), BF16),
            pltpu.VMEM((rows + 2 * HALO, width), F32),
            pltpu.VMEM((2, HALO, width), BF16),
            pltpu.VMEM((2, HALO, width), BF16),
            pltpu.SemaphoreType.DMA((5,)),
            pltpu.SemaphoreType.DMA((pairs,)),
            pltpu.SemaphoreType.DMA((pairs,)),
        ],
        compiler_params=pltpu.CompilerParams(
            collective_id=0, has_side_effects=True, vmem_limit_bytes=44 * 2**20
        ),
        cost_estimate=pl.CostEstimate(
            flops=2 * rows * d_model * (2 * hidden + 4 * width) + 8 * rows * rows * 4 * width,
            bytes_accessed=12 * 2**20,
            transcendentals=rows * rows * 24,
        ),
        name="conformer_block",
    )(
        left_groups, start_offset, frames, ffn_gain.reshape(1, -1), w_up, w_down,
        ln_gain.reshape(1, -1), w_qkv.reshape(d_model, 3 * width), w_out, conv_kernel,
    )


def solution(mesh):
    return jax.shard_map(
        body,
        mesh=mesh,
        in_specs=(
            P("tm", "mp"),
            P(),
            P(None, "mp"),
            P("mp", None),
            P(),
            P(None, None, "mp"),
            P("mp", None),
            P(None, "mp"),
            P("tm"),
            P("tm"),
        ),
        out_specs=P("tm", "mp"),
        check_vma=False,
    )
```

```python
import functools

import jax
import jax.numpy as jnp
from jax import lax
from jax.experimental import pallas as pl
from jax.experimental.pallas import tpu as pltpu
from jax.sharding import PartitionSpec as P

HEAD_DIM = 64
KERNEL = 31
LEFT = 3
REC_SHARDS = 8
CHUNKS = 4
FFN_CHUNKS = 2
LANES = 128
HALO = 16
HIDDEN_STEP = 256
NEVER = -1e30
F32 = jnp.float32
BF16 = jnp.bfloat16


def layer_norm(values_in, gain):
    widened = values_in.astype(F32)
    center = jnp.mean(widened, axis=-1, keepdims=True)
    shifted = widened - center
    spread = jnp.mean(shifted * shifted, axis=-1, keepdims=True)
    return (shifted * lax.rsqrt(spread + 1e-05) * gain).astype(BF16)


def dot(a, b, dims=((1,), (0,))):
    return lax.dot_general(a, b, (dims, ((), ())), preferred_element_type=F32)


def block_kernel(
    left_ref, offset_ref, frames, ffn_gain, w_up, w_down, ln_gain, w_qkv, w_out, taps, out,
    whole, up_v, down_v, qkv_v, out_v, hidden, normed, partial, partial_in, chip_out, chip_in,
    ffn_mid, queries, keys, values, scores, context, proj, proj_in, cross_out, cross_in, padded,
    edge_out, edge_in, local_sem, send_sem, recv_sem,
):
    rows, width = frames.shape
    d_model = whole.shape[1]
    size = rows // CHUNKS
    half = size // 2
    groups = lax.axis_size("tm")
    group = lax.axis_index("tm")
    me = lax.axis_index("mp")
    core = lax.rem(me, 2)
    side = me // 2
    sibling = me + 1 - 2 * core
    partner = lax.rem(me + 2, 4)
    following = lax.rem(group + 1, groups)
    previous = lax.rem(group + groups - 1, groups)

    loads = []
    for i, (src, dst) in enumerate(
        ((w_up, up_v), (w_down, down_v), (w_qkv, qkv_v), (w_out, out_v))
    ):
        loads.append(pltpu.make_async_copy(src, dst, local_sem.at[i]))
    own_cols = pl.ds(pl.multiple_of(me * width, LANES), width)
    own_frames = pltpu.make_async_copy(frames, whole.at[:, own_cols], local_sem.at[4])
    own_frames.start()
    for load in loads:
        load.start()

    barrier = pltpu.get_barrier_semaphore()
    for target in ({"mp": sibling}, {"mp": partner}, {"tm": following}, {"tm": previous}):
        pl.semaphore_signal(
            barrier, inc=1, device_id=target, device_id_type=pl.DeviceIdType.MESH
        )
    pl.semaphore_wait(barrier, 4)

    copies = []

    def send(src, dst, target):
        i = len(copies)
        copy = pltpu.make_async_remote_copy(
            src_ref=src, dst_ref=dst, send_sem=send_sem.at[i], recv_sem=recv_sem.at[i],
            device_id=target, device_id_type=pl.DeviceIdType.MESH,
        )
        copies.append(copy)
        copy.start()
        return copy

    def span(r):
        return pl.ds(r * size, size)

    def shared(r):
        return pl.ds(pl.multiple_of(r * size + core * half, half), half)

    per = CHUNKS // FFN_CHUNKS
    tall = per * size

    def wide(a):
        return pl.ds(a * tall, tall)

    to_partner, to_sibling = [], []
    for a in range(FFN_CHUNKS):
        to_partner.append(
            send(frames.at[wide(a), :], whole.at[wide(a), own_cols], {"mp": partner})
        )
        to_sibling.append(
            send(frames.at[wide(a), :], whole.at[wide(a), own_cols], {"mp": sibling})
        )
    own_frames.wait()

    partner_cols = pl.ds(pl.multiple_of(partner * width, LANES), width)
    mine = pl.ds(pl.multiple_of(core * half, half), half)
    theirs = pl.ds(pl.multiple_of((1 - core) * half, half), half)
    crossing = []
    for a in range(FFN_CHUNKS):
        to_partner[a].wait_recv()
        passed_on = send(
            whole.at[wide(a), partner_cols], whole.at[wide(a), partner_cols], {"mp": sibling}
        )
        to_sibling[a].wait_recv()
        passed_on.wait_recv()
        normed[...] = layer_norm(whole[wide(a), :], ffn_gain[...])
        if a == 0:
            loads[0].wait()

        @pl.loop(0, up_v.shape[1] // HIDDEN_STEP)
        def _(j):
            cols = pl.ds(pl.multiple_of(j * HIDDEN_STEP, HIDDEN_STEP), HIDDEN_STEP)
            v = dot(normed[...], up_v[:, cols])
            hidden[:, cols] = (v / (1.0 + jnp.exp(-v))).astype(BF16)

        if a == 0:
            loads[1].wait()

        @pl.loop(0, d_model // HIDDEN_STEP)
        def _(j):
            cols = pl.ds(pl.multiple_of(j * HIDDEN_STEP, HIDDEN_STEP), HIDDEN_STEP)
            product = dot(hidden[...], down_v[:, cols]).astype(BF16)
            for i in range(per):
                partial[a * per + i, :, cols] = product[i * size : (i + 1) * size]

        both = pl.ds(a * per, per)
        swap = send(partial.at[both, theirs, :], partial_in.at[both], {"mp": sibling})
        swap.wait_recv()
        for r in range(a * per, (a + 1) * per):
            chip_out[r] = (
                partial[r, mine, :].astype(F32) + partial_in[r].astype(F32)
            ).astype(BF16)
            crossing.append(send(chip_out.at[r], chip_in.at[r], {"mp": partner}))

    hops, here = {}, set()

    def arrive(part, h, r):
        if (part, h, r) not in here:
            here.add((part, h, r))
            hops[part, h, r].wait_recv()

    def hop(part, h, r):
        if h > 1:
            arrive(part, h - 1, r)
        held = (keys, values)[part]
        hops[part, h, r] = send(
            held.at[h - 1, span(r), :], held.at[h, span(r), :], {"tm": following}
        )

    for r in range(CHUNKS):
        crossing[r].wait_recv()
        total = chip_out[r].astype(F32) + chip_in[r].astype(F32)
        ffn_mid[shared(r), :] = (whole[shared(r), :].astype(F32) + 0.5 * total).astype(BF16)
        joined = send(ffn_mid.at[shared(r), :], ffn_mid.at[shared(r), :], {"mp": sibling})
        joined.wait_recv()
        ready = layer_norm(ffn_mid[span(r), :], ln_gain[...])
        normed[:size] = ready
        if r == 0:
            loads[2].wait()
        for part in range(2):
            (keys, values)[part][0, span(r), :] = dot(normed[:size], qkv_v[1 + part]).astype(BF16)
            hop(part, 1, r)
        queries[span(r), :] = (
            dot(normed[:size], qkv_v[0]).astype(BF16) * (HEAD_DIM ** -0.5)
        ).astype(BF16)
        if r < CHUNKS - 1:
            for h in range(LEFT, 1, -1):
                if r - h + 1 >= 0:
                    for part in range(2):
                        hop(part, h, r - h + 1)

    left = left_ref[0]
    offset = offset_ref[0]
    position = lax.broadcasted_iota(jnp.int32, (rows, rows), 1)
    upper = lax.broadcasted_iota(jnp.int32, (rows, LANES), 1) >= HEAD_DIM

    def score(d):
        if d > 0:
            first = jnp.where(d < left, 0, jnp.where(d == left, offset, rows))
            shown = position >= first

        @pl.loop(0, width // LANES)
        def _(p):
            cols = pl.ds(pl.multiple_of(p * LANES, LANES), LANES)
            pair = queries[:, cols]
            seen = keys[d, :, cols]
            for odd in range(2):
                picked = jnp.where(upper if odd else jnp.logical_not(upper), pair, 0)
                s = dot(picked, seen, ((1,), (1,)))
                if d > 0:
                    s = jnp.where(shown, s, NEVER)
                scores[2 * p + odd, :, d * rows : (d + 1) * rows] = s

    last = CHUNKS - 1
    stages = {1: ((3, last - 2), (2, last - 1), (2, last)), 2: ((3, last - 1), (3, last)), 3: ()}
    score(0)
    for d in range(1, LEFT + 1):
        for h, r in stages[d]:
            for part in range(2):
                hop(part, h, r)
        for r in range(CHUNKS):
            arrive(0, d, r)
        score(d)
    for d in range(1, LEFT + 1):
        for r in range(CHUNKS):
            arrive(1, d, r)

    lower = lax.broadcasted_iota(jnp.int32, (size, LANES), 1) < HEAD_DIM
    swaps, outgoing = {}, {}
    loads[3].wait()
    far = 1 - side

    def attend(r):
        @pl.loop(0, width // LANES)
        def _(p):
            cols = pl.ds(pl.multiple_of(p * LANES, LANES), LANES)
            found = []
            for odd in range(2):
                s = scores[2 * p + odd, span(r), :]
                e = jnp.exp(s - jnp.max(s, axis=-1, keepdims=True))
                norm = jnp.sum(e, axis=-1, keepdims=True)
                e = e.astype(BF16)
                acc = None
                for d in range(LEFT + 1):
                    term = dot(e[:, d * rows : (d + 1) * rows], values[d, :, cols])
                    acc = term if acc is None else acc + term
                found.append(acc / norm)
            context[span(r), cols] = jnp.where(lower, found[0], found[1]).astype(BF16)

        for k in range(4):
            proj[r, (k % 2) * 2 + k // 2] = dot(
                context[span(r), :], out_v[:, k * width : (k + 1) * width]
            ).astype(BF16)
        swaps[r] = send(proj.at[r, pl.ds((1 - core) * 2, 2)], proj_in.at[r], {"mp": sibling})

    def cross(r):
        swaps[r].wait_recv()
        cross_out[r] = (
            proj[r, core * 2 + far].astype(F32) + proj_in[r, far].astype(F32)
        ).astype(BF16)
        outgoing[r] = send(cross_out.at[r], cross_in.at[r], {"mp": partner})

    order = [0, CHUNKS - 1] + list(range(1, CHUNKS - 1))
    for i, r in enumerate(order):
        attend(r)
        if i:
            cross(order[i - 1])
    cross(order[-1])

    for r in order:
        own = (
            ffn_mid[span(r), own_cols].astype(F32)
            + proj[r, core * 2 + side].astype(F32)
            + proj_in[r, side].astype(F32)
        )
        outgoing[r].wait_recv()
        mid = (own + cross_in[r].astype(F32)).astype(BF16)
        padded[HALO + r * size : HALO + (r + 1) * size, :] = mid.astype(F32)
        if r == 0:
            edge_out[0] = mid[:HALO]
            back = send(edge_out.at[0], edge_in.at[0], {"tm": previous})
        if r == CHUNKS - 1:
            edge_out[1] = mid[size - HALO :]
            ahead = send(edge_out.at[1], edge_in.at[1], {"tm": following})
    place = lax.rem(group, REC_SHARDS)
    starts = jnp.logical_or(place == REC_SHARDS // 2, group == 0)
    ends = jnp.logical_or(place == REC_SHARDS // 2 - 1, group == groups - 1)
    back.wait_recv()
    padded[HALO + rows :, :] = edge_in[0].astype(F32) * jnp.where(ends, 0.0, 1.0)
    ahead.wait_recv()
    padded[:HALO, :] = edge_in[1].astype(F32) * jnp.where(starts, 0.0, 1.0)

    block = min(64, rows)
    for c in range(width // LANES):
        cols = slice(c * LANES, (c + 1) * LANES)

        @pl.loop(0, rows // block)
        def _(i):
            base = pl.multiple_of(i * block, block)
            near = padded[pl.ds(base, block + 2 * HALO), cols]
            total = jnp.zeros((block, LANES), F32)
            for shift in range(8):
                moved = near
                if shift:
                    moved = pltpu.roll(near, block + 2 * HALO - shift, 0)
                for up in range(0, 2 * HALO, 8):
                    tap = up + shift - 1
                    if 0 <= tap < KERNEL:
                        total = total + taps[tap : tap + 1, cols] * moved[up : up + block]
            mid = near[HALO : HALO + block]
            out[pl.ds(base, block), cols] = (
                mid + total / (1.0 + jnp.exp(-total))
            ).astype(BF16)

    for copy in copies:
        copy.wait_send()


def body(
    frames, ffn_gain, w_up, w_down, ln_gain, w_qkv, w_out, conv_kernel, left_groups, start_offset
):
    rows, width = frames.shape
    d_model = w_up.shape[0]
    hidden = w_up.shape[1]
    size = rows // CHUNKS
    pairs = 4 * FFN_CHUNKS + CHUNKS * (1 + 1 + 2 * LEFT + 1 + 1) + 2
    anywhere = pl.BlockSpec(memory_space=pl.ANY)
    in_vmem = pl.BlockSpec(memory_space=pltpu.VMEM)
    in_smem = pl.BlockSpec(memory_space=pltpu.SMEM)
    return pl.pallas_call(
        block_kernel,
        out_shape=jax.ShapeDtypeStruct((rows, width), BF16),
        in_specs=[
            in_smem, in_smem, anywhere, in_vmem, anywhere, anywhere, in_vmem, anywhere, anywhere,
            in_vmem,
        ],
        out_specs=in_vmem,
        scratch_shapes=[
            pltpu.VMEM((rows, d_model), BF16),
            pltpu.VMEM(w_up.shape, BF16),
            pltpu.VMEM(w_down.shape, BF16),
            pltpu.VMEM((3, d_model, width), BF16),
            pltpu.VMEM(w_out.shape, BF16),
            pltpu.VMEM((rows // FFN_CHUNKS, hidden), BF16),
            pltpu.VMEM((rows // FFN_CHUNKS, d_model), BF16),
            pltpu.VMEM((CHUNKS, size, d_model), BF16),
            pltpu.VMEM((CHUNKS, size // 2, d_model), BF16),
            pltpu.VMEM((CHUNKS, size // 2, d_model), BF16),
            pltpu.VMEM((CHUNKS, size // 2, d_model), BF16),
            pltpu.VMEM((rows, d_model), BF16),
            pltpu.VMEM((rows, width), BF16),
            pltpu.VMEM((LEFT + 1, rows, width), BF16),
            pltpu.VMEM((LEFT + 1, rows, width), BF16),
            pltpu.VMEM((width // HEAD_DIM, rows, (LEFT + 1) * rows), F32),
            pltpu.VMEM((rows, width), BF16),
            pltpu.VMEM((CHUNKS, 4, size, width), BF16),
            pltpu.VMEM((CHUNKS, 2, size, width), BF16),
            pltpu.VMEM((CHUNKS, size, width), BF16),
            pltpu.VMEM((CHUNKS, size, width), BF16),
            pltpu.VMEM((rows + 2 * HALO, width), F32),
            pltpu.VMEM((2, HALO, width), BF16),
            pltpu.VMEM((2, HALO, width), BF16),
            pltpu.SemaphoreType.DMA((5,)),
            pltpu.SemaphoreType.DMA((pairs,)),
            pltpu.SemaphoreType.DMA((pairs,)),
        ],
        compiler_params=pltpu.CompilerParams(
            collective_id=0, has_side_effects=True, vmem_limit_bytes=60 * 2**20
        ),
        cost_estimate=pl.CostEstimate(
            flops=2 * rows * d_model * (2 * hidden + 4 * width) + 8 * rows * rows * 4 * width,
            bytes_accessed=12 * 2**20,
            transcendentals=rows * rows * 24,
        ),
        name="conformer_block",
    )(
        left_groups, start_offset, frames, ffn_gain.reshape(1, -1), w_up, w_down,
        ln_gain.reshape(1, -1), jnp.transpose(w_qkv, (1, 0, 2)), w_out, conv_kernel,
    )


def solution(mesh):
    return jax.shard_map(
        body,
        mesh=mesh,
        in_specs=(
            P("tm", "mp"),
            P(),
            P(None, "mp"),
            P("mp", None),
            P(),
            P(None, None, "mp"),
            P("mp", None),
            P(None, "mp"),
            P("tm"),
            P("tm"),
        ),
        out_specs=P("tm", "mp"),
        check_vma=False,
    )
```

```python
import functools

import jax
import jax.numpy as jnp
from jax import lax
from jax.experimental import pallas as pl
from jax.experimental.pallas import tpu as pltpu
from jax.sharding import PartitionSpec as P

HEAD_DIM = 64
KERNEL = 31
LEFT = 3
REC_SHARDS = 8
CHUNKS = 4
FFN_CHUNKS = 4
LANES = 128
HALO = 16
HIDDEN_STEP = 256
NEVER = -1e30
F32 = jnp.float32
BF16 = jnp.bfloat16


def layer_norm(values_in, gain):
    widened = values_in.astype(F32)
    center = jnp.mean(widened, axis=-1, keepdims=True)
    shifted = widened - center
    spread = jnp.mean(shifted * shifted, axis=-1, keepdims=True)
    return (shifted * lax.rsqrt(spread + 1e-05) * gain).astype(BF16)


def dot(a, b, dims=((1,), (0,))):
    return lax.dot_general(a, b, (dims, ((), ())), preferred_element_type=F32)


def block_kernel(
    left_ref, offset_ref, frames, ffn_gain_in, w_up, w_down, ln_gain_in, w_qkv, w_out, taps_in, out,
    whole, up_v, down_v, qkv_v, out_v, hidden, normed, partial, partial_in, chip_out, chip_in,
    ffn_mid, queries, keys, values, scores, context, proj, proj_in, cross_out, cross_in, padded,
    edge_out, edge_in, ffn_gain, ln_gain, taps, local_sem, send_sem, recv_sem,
):
    rows, width = frames.shape
    d_model = whole.shape[1]
    size = rows // CHUNKS
    half = size // 2
    groups = lax.axis_size("tm")
    group = lax.axis_index("tm")
    me = lax.axis_index("mp")
    core = lax.rem(me, 2)
    side = me // 2
    sibling = me + 1 - 2 * core
    partner = lax.rem(me + 2, 4)
    following = lax.rem(group + 1, groups)
    previous = lax.rem(group + groups - 1, groups)

    barrier = pltpu.get_barrier_semaphore()
    for target in ({"mp": sibling}, {"mp": partner}, {"tm": following}, {"tm": previous}):
        pl.semaphore_signal(
            barrier, inc=1, device_id=target, device_id_type=pl.DeviceIdType.MESH
        )

    loads = []
    for i, (src, dst) in enumerate(
        (
            (w_up, up_v), (w_down, down_v), (w_qkv, qkv_v), (w_out, out_v),
            (ffn_gain_in, ffn_gain), (ln_gain_in, ln_gain), (taps_in, taps),
        )
    ):
        loads.append(pltpu.make_async_copy(src, dst, local_sem.at[i]))
    own_cols = pl.ds(pl.multiple_of(me * width, LANES), width)
    own_frames = pltpu.make_async_copy(frames, whole.at[:, own_cols], local_sem.at[7])
    own_frames.start()
    loads[4].start()
    for load in loads[:4] + loads[5:]:
        load.start()

    pl.semaphore_wait(barrier, 4)

    copies = []

    def send(src, dst, target):
        i = len(copies)
        copy = pltpu.make_async_remote_copy(
            src_ref=src, dst_ref=dst, send_sem=send_sem.at[i], recv_sem=recv_sem.at[i],
            device_id=target, device_id_type=pl.DeviceIdType.MESH,
        )
        copies.append(copy)
        copy.start()
        return copy

    def span(r):
        return pl.ds(r * size, size)

    def shared(r):
        return pl.ds(pl.multiple_of(r * size + core * half, half), half)

    per = CHUNKS // FFN_CHUNKS
    tall = per * size

    def wide(a):
        return pl.ds(a * tall, tall)

    to_partner, to_sibling = [], []
    for a in range(FFN_CHUNKS):
        to_partner.append(
            send(frames.at[wide(a), :], whole.at[wide(a), own_cols], {"mp": partner})
        )
        to_sibling.append(
            send(frames.at[wide(a), :], whole.at[wide(a), own_cols], {"mp": sibling})
        )
    own_frames.wait()

    partner_cols = pl.ds(pl.multiple_of(partner * width, LANES), width)
    mine = pl.ds(pl.multiple_of(core * half, half), half)
    theirs = pl.ds(pl.multiple_of((1 - core) * half, half), half)
    crossing, given = [], []

    def exchange(a):
        given[a].wait_recv()
        for r in range(a * per, (a + 1) * per):
            chip_out[r] = (
                partial[r, mine, :].astype(F32) + partial_in[r].astype(F32)
            ).astype(BF16)
            crossing.append(send(chip_out.at[r], chip_in.at[r], {"mp": partner}))

    for a in range(FFN_CHUNKS):
        to_partner[a].wait_recv()
        passed_on = send(
            whole.at[wide(a), partner_cols], whole.at[wide(a), partner_cols], {"mp": sibling}
        )
        to_sibling[a].wait_recv()
        passed_on.wait_recv()
        if a == 0:
            loads[4].wait()
        normed[...] = layer_norm(whole[wide(a), :], ffn_gain[...].reshape(1, d_model))
        if a == 0:
            loads[0].wait()

        @pl.loop(0, up_v.shape[1] // HIDDEN_STEP)
        def _(j):
            cols = pl.ds(pl.multiple_of(j * HIDDEN_STEP, HIDDEN_STEP), HIDDEN_STEP)
            v = dot(normed[...], up_v[:, cols])
            hidden[:, cols] = (v / (1.0 + jnp.exp(-v))).astype(BF16)

        if a == 0:
            loads[1].wait()

        @pl.loop(0, d_model // HIDDEN_STEP)
        def _(j):
            cols = pl.ds(pl.multiple_of(j * HIDDEN_STEP, HIDDEN_STEP), HIDDEN_STEP)
            product = dot(hidden[...], down_v[:, cols]).astype(BF16)
            for i in range(per):
                partial[a * per + i, :, cols] = product[i * size : (i + 1) * size]

        both = pl.ds(a * per, per)
        given.append(send(partial.at[both, theirs, :], partial_in.at[both], {"mp": sibling}))
        if a:
            exchange(a - 1)
    exchange(FFN_CHUNKS - 1)

    hops, here = {}, set()

    def arrive(part, h, r):
        if (part, h, r) not in here:
            here.add((part, h, r))
            hops[part, h, r].wait_recv()

    def hop(part, h, r):
        if h > 1:
            arrive(part, h - 1, r)
        held = (keys, values)[part]
        hops[part, h, r] = send(
            held.at[h - 1, span(r), :], held.at[h, span(r), :], {"tm": following}
        )

    for r in range(CHUNKS):
        crossing[r].wait_recv()
        total = chip_out[r].astype(F32) + chip_in[r].astype(F32)
        ffn_mid[shared(r), :] = (whole[shared(r), :].astype(F32) + 0.5 * total).astype(BF16)
        joined = send(ffn_mid.at[shared(r), :], ffn_mid.at[shared(r), :], {"mp": sibling})
        joined.wait_recv()
        if r == 0:
            loads[5].wait()
        ready = layer_norm(ffn_mid[span(r), :], ln_gain[...].reshape(1, d_model))
        normed[:size] = ready
        if r == 0:
            loads[2].wait()
        for part in range(2):
            (keys, values)[part][0, span(r), :] = dot(normed[:size], qkv_v[1 + part]).astype(BF16)
            hop(part, 1, r)
        queries[span(r), :] = (
            dot(normed[:size], qkv_v[0]).astype(BF16) * (HEAD_DIM ** -0.5)
        ).astype(BF16)
        if r < CHUNKS - 1:
            for h in range(LEFT, 1, -1):
                if r - h + 1 >= 0:
                    for part in range(2):
                        hop(part, h, r - h + 1)

    left = left_ref[0]
    offset = offset_ref[0]
    position = lax.broadcasted_iota(jnp.int32, (rows, rows), 1)
    upper = lax.broadcasted_iota(jnp.int32, (rows, LANES), 1) >= HEAD_DIM

    def score(d):
        if d > 0:
            first = jnp.where(d < left, 0, jnp.where(d == left, offset, rows))
            shown = position >= first

        @pl.loop(0, width // LANES)
        def _(p):
            cols = pl.ds(pl.multiple_of(p * LANES, LANES), LANES)
            pair = queries[:, cols]
            seen = keys[d, :, cols]
            for odd in range(2):
                picked = jnp.where(upper if odd else jnp.logical_not(upper), pair, 0)
                s = dot(picked, seen, ((1,), (1,)))
                if d > 0:
                    s = jnp.where(shown, s, NEVER)
                scores[2 * p + odd, :, d * rows : (d + 1) * rows] = s

    last = CHUNKS - 1
    stages = {1: ((3, last - 2), (2, last - 1), (2, last)), 2: ((3, last - 1), (3, last)), 3: ()}
    score(0)
    for d in range(1, LEFT + 1):
        for h, r in stages[d]:
            for part in range(2):
                hop(part, h, r)
        for r in range(CHUNKS):
            arrive(0, d, r)
        score(d)
    for d in range(1, LEFT + 1):
        for r in range(CHUNKS):
            arrive(1, d, r)

    lower = lax.broadcasted_iota(jnp.int32, (size, LANES), 1) < HEAD_DIM
    swaps, outgoing = {}, {}
    loads[3].wait()
    far = 1 - side

    def attend(r):
        @pl.loop(0, width // LANES)
        def _(p):
            cols = pl.ds(pl.multiple_of(p * LANES, LANES), LANES)
            found = []
            for odd in range(2):
                s = scores[2 * p + odd, span(r), :]
                e = jnp.exp(s - jnp.max(s, axis=-1, keepdims=True))
                norm = jnp.sum(e, axis=-1, keepdims=True)
                e = e.astype(BF16)
                acc = None
                for d in range(LEFT + 1):
                    term = dot(e[:, d * rows : (d + 1) * rows], values[d, :, cols])
                    acc = term if acc is None else acc + term
                found.append(acc / norm)
            context[span(r), cols] = jnp.where(lower, found[0], found[1]).astype(BF16)

        for k in range(4):
            proj[r, (k % 2) * 2 + k // 2] = dot(
                context[span(r), :], out_v[:, k * width : (k + 1) * width]
            ).astype(BF16)
        swaps[r] = send(proj.at[r, pl.ds((1 - core) * 2, 2)], proj_in.at[r], {"mp": sibling})

    def cross(r):
        swaps[r].wait_recv()
        cross_out[r] = (
            proj[r, core * 2 + far].astype(F32) + proj_in[r, far].astype(F32)
        ).astype(BF16)
        outgoing[r] = send(cross_out.at[r], cross_in.at[r], {"mp": partner})

    order = [0, CHUNKS - 1] + list(range(1, CHUNKS - 1))
    for i, r in enumerate(order):
        attend(r)
        if i:
            cross(order[i - 1])
    cross(order[-1])

    for r in order:
        own = (
            ffn_mid[span(r), own_cols].astype(F32)
            + proj[r, core * 2 + side].astype(F32)
            + proj_in[r, side].astype(F32)
        )
        outgoing[r].wait_recv()
        mid = (own + cross_in[r].astype(F32)).astype(BF16)
        padded[HALO + r * size : HALO + (r + 1) * size, :] = mid.astype(F32)
        if r == 0:
            edge_out[0] = mid[:HALO]
            back = send(edge_out.at[0], edge_in.at[0], {"tm": previous})
        if r == CHUNKS - 1:
            edge_out[1] = mid[size - HALO :]
            ahead = send(edge_out.at[1], edge_in.at[1], {"tm": following})
    loads[6].wait()
    place = lax.rem(group, REC_SHARDS)
    starts = jnp.logical_or(place == REC_SHARDS // 2, group == 0)
    ends = jnp.logical_or(place == REC_SHARDS // 2 - 1, group == groups - 1)
    back.wait_recv()
    padded[HALO + rows :, :] = edge_in[0].astype(F32) * jnp.where(ends, 0.0, 1.0)
    ahead.wait_recv()
    padded[:HALO, :] = edge_in[1].astype(F32) * jnp.where(starts, 0.0, 1.0)

    block = min(64, rows)
    for c in range(width // LANES):
        cols = slice(c * LANES, (c + 1) * LANES)

        @pl.loop(0, rows // block)
        def _(i):
            base = pl.multiple_of(i * block, block)
            near = padded[pl.ds(base, block + 2 * HALO), cols]
            total = jnp.zeros((block, LANES), F32)
            for shift in range(8):
                moved = near
                if shift:
                    moved = pltpu.roll(near, block + 2 * HALO - shift, 0)
                for up in range(0, 2 * HALO, 8):
                    tap = up + shift - 1
                    if 0 <= tap < KERNEL:
                        total = total + taps[tap : tap + 1, cols] * moved[up : up + block]
            mid = near[HALO : HALO + block]
            out[pl.ds(base, block), cols] = (
                mid + total / (1.0 + jnp.exp(-total))
            ).astype(BF16)

    for copy in copies:
        copy.wait_send()


def body(
    frames, ffn_gain, w_up, w_down, ln_gain, w_qkv, w_out, conv_kernel, left_groups, start_offset
):
    rows, width = frames.shape
    d_model = w_up.shape[0]
    hidden = w_up.shape[1]
    size = rows // CHUNKS
    pairs = 4 * FFN_CHUNKS + CHUNKS * (1 + 1 + 2 * LEFT + 1 + 1) + 2
    anywhere = pl.BlockSpec(memory_space=pl.ANY)
    in_vmem = pl.BlockSpec(memory_space=pltpu.VMEM)
    in_smem = pl.BlockSpec(memory_space=pltpu.SMEM)
    return pl.pallas_call(
        block_kernel,
        out_shape=jax.ShapeDtypeStruct((rows, width), BF16),
        in_specs=[
            in_smem, in_smem, anywhere, anywhere, anywhere, anywhere, anywhere, anywhere, anywhere,
            anywhere,
        ],
        out_specs=in_vmem,
        scratch_shapes=[
            pltpu.VMEM((rows, d_model), BF16),
            pltpu.VMEM(w_up.shape, BF16),
            pltpu.VMEM(w_down.shape, BF16),
            pltpu.VMEM((3, d_model, width), BF16),
            pltpu.VMEM(w_out.shape, BF16),
            pltpu.VMEM((rows // FFN_CHUNKS, hidden), BF16),
            pltpu.VMEM((rows // FFN_CHUNKS, d_model), BF16),
            pltpu.VMEM((CHUNKS, size, d_model), BF16),
            pltpu.VMEM((CHUNKS, size // 2, d_model), BF16),
            pltpu.VMEM((CHUNKS, size // 2, d_model), BF16),
            pltpu.VMEM((CHUNKS, size // 2, d_model), BF16),
            pltpu.VMEM((rows, d_model), BF16),
            pltpu.VMEM((rows, width), BF16),
            pltpu.VMEM((LEFT + 1, rows, width), BF16),
            pltpu.VMEM((LEFT + 1, rows, width), BF16),
            pltpu.VMEM((width // HEAD_DIM, rows, (LEFT + 1) * rows), F32),
            pltpu.VMEM((rows, width), BF16),
            pltpu.VMEM((CHUNKS, 4, size, width), BF16),
            pltpu.VMEM((CHUNKS, 2, size, width), BF16),
            pltpu.VMEM((CHUNKS, size, width), BF16),
            pltpu.VMEM((CHUNKS, size, width), BF16),
            pltpu.VMEM((rows + 2 * HALO, width), F32),
            pltpu.VMEM((2, HALO, width), BF16),
            pltpu.VMEM((2, HALO, width), BF16),
            pltpu.VMEM((d_model,), F32),
            pltpu.VMEM((d_model,), F32),
            pltpu.VMEM((KERNEL, width), F32),
            pltpu.SemaphoreType.DMA((8,)),
            pltpu.SemaphoreType.DMA((pairs,)),
            pltpu.SemaphoreType.DMA((pairs,)),
        ],
        compiler_params=pltpu.CompilerParams(
            collective_id=0, has_side_effects=True, vmem_limit_bytes=60 * 2**20
        ),
        cost_estimate=pl.CostEstimate(
            flops=2 * rows * d_model * (2 * hidden + 4 * width) + 8 * rows * rows * 4 * width,
            bytes_accessed=12 * 2**20,
            transcendentals=rows * rows * 24,
        ),
        name="conformer_block",
    )(
        left_groups, start_offset, frames, ffn_gain, w_up, w_down,
        ln_gain, jnp.transpose(w_qkv, (1, 0, 2)), w_out, conv_kernel,
    )


def solution(mesh):
    return jax.shard_map(
        body,
        mesh=mesh,
        in_specs=(
            P("tm", "mp"),
            P(),
            P(None, "mp"),
            P("mp", None),
            P(),
            P(None, None, "mp"),
            P("mp", None),
            P(None, "mp"),
            P("tm"),
            P("tm"),
        ),
        out_specs=P("tm", "mp"),
        check_vma=False,
    )
```

```python
import functools

import jax
import jax.numpy as jnp
from jax import lax
from jax.experimental import pallas as pl
from jax.experimental.pallas import tpu as pltpu
from jax.sharding import PartitionSpec as P

HEAD_DIM = 64
KERNEL = 31
LEFT = 3
REC_SHARDS = 8
CHUNKS = 4
FFN_CHUNKS = 4
LANES = 128
HALO = 16
HIDDEN_STEP = 256
NEVER = -1e30
F32 = jnp.float32
BF16 = jnp.bfloat16


def layer_norm(values_in, gain):
    widened = values_in.astype(F32)
    center = jnp.mean(widened, axis=-1, keepdims=True)
    shifted = widened - center
    spread = jnp.mean(shifted * shifted, axis=-1, keepdims=True)
    return (shifted * lax.rsqrt(spread + 1e-05) * gain).astype(BF16)


def dot(a, b, dims=((1,), (0,))):
    return lax.dot_general(a, b, (dims, ((), ())), preferred_element_type=F32)


def block_kernel(
    left_ref, offset_ref, frames, ffn_gain_in, w_up, w_down, ln_gain_in, w_qkv, w_out, taps_in, out,
    whole, up_v, down_v, qkv_v, out_v, hidden, normed, partial, partial_in, chip_out, chip_in,
    ffn_mid, queries, keys, values, scores, context, proj, proj_in, cross_out, cross_in, padded,
    edge_out, edge_in, ffn_gain, ln_gain, taps, ready, local_sem, send_sem, recv_sem,
):
    rows, width = frames.shape
    d_model = whole.shape[1]
    size = rows // CHUNKS
    half = size // 2
    groups = lax.axis_size("tm")
    group = lax.axis_index("tm")
    me = lax.axis_index("mp")
    core = lax.rem(me, 2)
    side = me // 2
    sibling = me + 1 - 2 * core
    partner = lax.rem(me + 2, 4)
    following = lax.rem(group + 1, groups)
    previous = lax.rem(group + groups - 1, groups)

    barrier = pltpu.get_barrier_semaphore()
    for target in ({"mp": sibling}, {"mp": partner}, {"tm": following}, {"tm": previous}):
        pl.semaphore_signal(
            barrier, inc=1, device_id=target, device_id_type=pl.DeviceIdType.MESH
        )

    loads = []
    for i, (src, dst) in enumerate(
        (
            (w_up, up_v), (w_down, down_v), (w_qkv, qkv_v), (w_out, out_v),
            (ffn_gain_in, ffn_gain), (ln_gain_in, ln_gain), (taps_in, taps),
        )
    ):
        loads.append(pltpu.make_async_copy(src, dst, local_sem.at[i]))
    own_cols = pl.ds(pl.multiple_of(me * width, LANES), width)
    own_frames = pltpu.make_async_copy(frames, whole.at[:, own_cols], local_sem.at[7])
    own_frames.start()
    loads[4].start()
    for load in loads[:4] + loads[5:]:
        load.start()

    pl.semaphore_wait(barrier, 4)

    copies = []

    def send(src, dst, target):
        i = len(copies)
        copy = pltpu.make_async_remote_copy(
            src_ref=src, dst_ref=dst, send_sem=send_sem.at[i], recv_sem=recv_sem.at[i],
            device_id=target, device_id_type=pl.DeviceIdType.MESH,
        )
        copies.append(copy)
        copy.start()
        return copy

    def span(r):
        return pl.ds(r * size, size)

    def shared(r):
        return pl.ds(pl.multiple_of(r * size + core * half, half), half)

    per = CHUNKS // FFN_CHUNKS
    tall = per * size

    def wide(a):
        return pl.ds(a * tall, tall)

    to_partner, to_sibling = [], []
    for a in range(FFN_CHUNKS):
        to_partner.append(
            send(frames.at[wide(a), :], whole.at[wide(a), own_cols], {"mp": partner})
        )
        to_sibling.append(
            send(frames.at[wide(a), :], whole.at[wide(a), own_cols], {"mp": sibling})
        )
    own_frames.wait()

    partner_cols = pl.ds(pl.multiple_of(partner * width, LANES), width)
    mine = pl.ds(pl.multiple_of(core * half, half), half)
    theirs = pl.ds(pl.multiple_of((1 - core) * half, half), half)
    crossing, given = [], []

    def exchange(a):
        given[a].wait_recv()
        for r in range(a * per, (a + 1) * per):
            chip_out[r] = (
                partial[r, mine, :].astype(F32) + partial_in[r].astype(F32)
            ).astype(BF16)
            crossing.append(send(chip_out.at[r], chip_in.at[r], {"mp": partner}))

    for a in range(FFN_CHUNKS):
        to_partner[a].wait_recv()
        passed_on = send(
            whole.at[wide(a), partner_cols], whole.at[wide(a), partner_cols], {"mp": sibling}
        )
        to_sibling[a].wait_recv()
        passed_on.wait_recv()
        if a == 0:
            loads[4].wait()
        normed[...] = layer_norm(whole[wide(a), :], ffn_gain[...].reshape(1, d_model))
        if a == 0:
            loads[0].wait()

        @pl.loop(0, up_v.shape[1] // HIDDEN_STEP)
        def _(j):
            cols = pl.ds(pl.multiple_of(j * HIDDEN_STEP, HIDDEN_STEP), HIDDEN_STEP)
            v = dot(normed[...], up_v[:, cols])
            hidden[:, cols] = (v / (1.0 + jnp.exp(-v))).astype(BF16)

        if a == 0:
            loads[1].wait()

        @pl.loop(0, d_model // HIDDEN_STEP)
        def _(j):
            cols = pl.ds(pl.multiple_of(j * HIDDEN_STEP, HIDDEN_STEP), HIDDEN_STEP)
            product = dot(hidden[...], down_v[:, cols]).astype(BF16)
            for i in range(per):
                partial[a * per + i, :, cols] = product[i * size : (i + 1) * size]

        both = pl.ds(a * per, per)
        given.append(send(partial.at[both, theirs, :], partial_in.at[both], {"mp": sibling}))
        exchange(a)

    hops, here = {}, set()

    def arrive(part, h, r):
        if (part, h, r) not in here:
            here.add((part, h, r))
            hops[part, h, r].wait_recv()

    def hop(part, h, r):
        if h > 1:
            arrive(part, h - 1, r)
        held = (keys, values)[part]
        hops[part, h, r] = send(
            held.at[h - 1, span(r), :], held.at[h, span(r), :], {"tm": following}
        )

    def query(r):
        queries[span(r), :] = (
            dot(ready[span(r), :], qkv_v[0]).astype(BF16) * (HEAD_DIM ** -0.5)
        ).astype(BF16)

    for r in range(CHUNKS):
        crossing[r].wait_recv()
        total = chip_out[r].astype(F32) + chip_in[r].astype(F32)
        ffn_mid[shared(r), :] = (whole[shared(r), :].astype(F32) + 0.5 * total).astype(BF16)
        joined = send(ffn_mid.at[shared(r), :], ffn_mid.at[shared(r), :], {"mp": sibling})
        if r > 0:
            query(r - 1)
        joined.wait_recv()
        if r == 0:
            loads[5].wait()
        ready[span(r), :] = layer_norm(ffn_mid[span(r), :], ln_gain[...].reshape(1, d_model))
        if r == 0:
            loads[2].wait()
        for part in range(2):
            (keys, values)[part][0, span(r), :] = dot(ready[span(r), :], qkv_v[1 + part]).astype(BF16)
            hop(part, 1, r)
        if r < CHUNKS - 1:
            for h in range(LEFT, 1, -1):
                if r - h + 1 >= 0:
                    for part in range(2):
                        hop(part, h, r - h + 1)

    query(CHUNKS - 1)
    left = left_ref[0]
    offset = offset_ref[0]
    position = lax.broadcasted_iota(jnp.int32, (rows, rows), 1)
    upper = lax.broadcasted_iota(jnp.int32, (rows, LANES), 1) >= HEAD_DIM

    def score(d):
        if d > 0:
            first = jnp.where(d < left, 0, jnp.where(d == left, offset, rows))
            shown = position >= first

        @pl.loop(0, width // LANES)
        def _(p):
            cols = pl.ds(pl.multiple_of(p * LANES, LANES), LANES)
            pair = queries[:, cols]
            seen = keys[d, :, cols]
            for odd in range(2):
                picked = jnp.where(upper if odd else jnp.logical_not(upper), pair, 0)
                s = dot(picked, seen, ((1,), (1,)))
                if d > 0:
                    s = jnp.where(shown, s, NEVER)
                scores[2 * p + odd, :, d * rows : (d + 1) * rows] = s

    last = CHUNKS - 1
    stages = {1: ((3, last - 2), (2, last - 1), (2, last)), 2: ((3, last - 1), (3, last)), 3: ()}
    score(0)
    for d in range(1, LEFT + 1):
        for h, r in stages[d]:
            for part in range(2):
                hop(part, h, r)
        for r in range(CHUNKS):
            arrive(0, d, r)
        score(d)
    for d in range(1, LEFT + 1):
        for r in range(CHUNKS):
            arrive(1, d, r)

    lower = lax.broadcasted_iota(jnp.int32, (size, LANES), 1) < HEAD_DIM
    swaps, outgoing = {}, {}
    loads[3].wait()
    far = 1 - side

    def attend(r):
        @pl.loop(0, width // LANES)
        def _(p):
            cols = pl.ds(pl.multiple_of(p * LANES, LANES), LANES)
            found = []
            for odd in range(2):
                s = scores[2 * p + odd, span(r), :]
                e = jnp.exp(s - jnp.max(s, axis=-1, keepdims=True))
                norm = jnp.sum(e, axis=-1, keepdims=True)
                e = e.astype(BF16)
                acc = None
                for d in range(LEFT + 1):
                    term = dot(e[:, d * rows : (d + 1) * rows], values[d, :, cols])
                    acc = term if acc is None else acc + term
                found.append(acc / norm)
            context[span(r), cols] = jnp.where(lower, found[0], found[1]).astype(BF16)

        for k in range(4):
            proj[r, (k % 2) * 2 + k // 2] = dot(
                context[span(r), :], out_v[:, k * width : (k + 1) * width]
            ).astype(BF16)
        swaps[r] = send(proj.at[r, pl.ds((1 - core) * 2, 2)], proj_in.at[r], {"mp": sibling})

    def cross(r):
        swaps[r].wait_recv()
        cross_out[r] = (
            proj[r, core * 2 + far].astype(F32) + proj_in[r, far].astype(F32)
        ).astype(BF16)
        outgoing[r] = send(cross_out.at[r], cross_in.at[r], {"mp": partner})

    order = [0, CHUNKS - 1] + list(range(1, CHUNKS - 1))
    for i, r in enumerate(order):
        attend(r)
        if i:
            cross(order[i - 1])
    cross(order[-1])

    for r in order:
        own = (
            ffn_mid[span(r), own_cols].astype(F32)
            + proj[r, core * 2 + side].astype(F32)
            + proj_in[r, side].astype(F32)
        )
        outgoing[r].wait_recv()
        mid = (own + cross_in[r].astype(F32)).astype(BF16)
        padded[HALO + r * size : HALO + (r + 1) * size, :] = mid.astype(F32)
        if r == 0:
            edge_out[0] = mid[:HALO]
            back = send(edge_out.at[0], edge_in.at[0], {"tm": previous})
        if r == CHUNKS - 1:
            edge_out[1] = mid[size - HALO :]
            ahead = send(edge_out.at[1], edge_in.at[1], {"tm": following})
    loads[6].wait()
    place = lax.rem(group, REC_SHARDS)
    starts = jnp.logical_or(place == REC_SHARDS // 2, group == 0)
    ends = jnp.logical_or(place == REC_SHARDS // 2 - 1, group == groups - 1)
    back.wait_recv()
    padded[HALO + rows :, :] = edge_in[0].astype(F32) * jnp.where(ends, 0.0, 1.0)
    ahead.wait_recv()
    padded[:HALO, :] = edge_in[1].astype(F32) * jnp.where(starts, 0.0, 1.0)

    block = min(64, rows)
    for c in range(width // LANES):
        cols = slice(c * LANES, (c + 1) * LANES)

        @pl.loop(0, rows // block)
        def _(i):
            base = pl.multiple_of(i * block, block)
            near = padded[pl.ds(base, block + 2 * HALO), cols]
            total = jnp.zeros((block, LANES), F32)
            for shift in range(8):
                moved = near
                if shift:
                    moved = pltpu.roll(near, block + 2 * HALO - shift, 0)
                for up in range(0, 2 * HALO, 8):
                    tap = up + shift - 1
                    if 0 <= tap < KERNEL:
                        total = total + taps[tap : tap + 1, cols] * moved[up : up + block]
            mid = near[HALO : HALO + block]
            out[pl.ds(base, block), cols] = (
                mid + total / (1.0 + jnp.exp(-total))
            ).astype(BF16)

    for copy in copies:
        copy.wait_send()


def body(
    frames, ffn_gain, w_up, w_down, ln_gain, w_qkv, w_out, conv_kernel, left_groups, start_offset
):
    rows, width = frames.shape
    d_model = w_up.shape[0]
    hidden = w_up.shape[1]
    size = rows // CHUNKS
    pairs = 4 * FFN_CHUNKS + CHUNKS * (1 + 1 + 2 * LEFT + 1 + 1) + 2
    anywhere = pl.BlockSpec(memory_space=pl.ANY)
    in_vmem = pl.BlockSpec(memory_space=pltpu.VMEM)
    in_smem = pl.BlockSpec(memory_space=pltpu.SMEM)
    return pl.pallas_call(
        block_kernel,
        out_shape=jax.ShapeDtypeStruct((rows, width), BF16),
        in_specs=[
            in_smem, in_smem, anywhere, anywhere, anywhere, anywhere, anywhere, anywhere, anywhere,
            anywhere,
        ],
        out_specs=in_vmem,
        scratch_shapes=[
            pltpu.VMEM((rows, d_model), BF16),
            pltpu.VMEM(w_up.shape, BF16),
            pltpu.VMEM(w_down.shape, BF16),
            pltpu.VMEM((3, d_model, width), BF16),
            pltpu.VMEM(w_out.shape, BF16),
            pltpu.VMEM((rows // FFN_CHUNKS, hidden), BF16),
            pltpu.VMEM((rows // FFN_CHUNKS, d_model), BF16),
            pltpu.VMEM((CHUNKS, size, d_model), BF16),
            pltpu.VMEM((CHUNKS, size // 2, d_model), BF16),
            pltpu.VMEM((CHUNKS, size // 2, d_model), BF16),
            pltpu.VMEM((CHUNKS, size // 2, d_model), BF16),
            pltpu.VMEM((rows, d_model), BF16),
            pltpu.VMEM((rows, width), BF16),
            pltpu.VMEM((LEFT + 1, rows, width), BF16),
            pltpu.VMEM((LEFT + 1, rows, width), BF16),
            pltpu.VMEM((width // HEAD_DIM, rows, (LEFT + 1) * rows), F32),
            pltpu.VMEM((rows, width), BF16),
            pltpu.VMEM((CHUNKS, 4, size, width), BF16),
            pltpu.VMEM((CHUNKS, 2, size, width), BF16),
            pltpu.VMEM((CHUNKS, size, width), BF16),
            pltpu.VMEM((CHUNKS, size, width), BF16),
            pltpu.VMEM((rows + 2 * HALO, width), F32),
            pltpu.VMEM((2, HALO, width), BF16),
            pltpu.VMEM((2, HALO, width), BF16),
            pltpu.VMEM((d_model,), F32),
            pltpu.VMEM((d_model,), F32),
            pltpu.VMEM((KERNEL, width), F32),
            pltpu.VMEM((rows, d_model), BF16),
            pltpu.SemaphoreType.DMA((8,)),
            pltpu.SemaphoreType.DMA((pairs,)),
            pltpu.SemaphoreType.DMA((pairs,)),
        ],
        compiler_params=pltpu.CompilerParams(
            collective_id=0, has_side_effects=True, vmem_limit_bytes=60 * 2**20
        ),
        cost_estimate=pl.CostEstimate(
            flops=2 * rows * d_model * (2 * hidden + 4 * width) + 8 * rows * rows * 4 * width,
            bytes_accessed=12 * 2**20,
            transcendentals=rows * rows * 24,
        ),
        name="conformer_block",
    )(
        left_groups, start_offset, frames, ffn_gain, w_up, w_down,
        ln_gain, jnp.transpose(w_qkv, (1, 0, 2)), w_out, conv_kernel,
    )


def solution(mesh):
    return jax.shard_map(
        body,
        mesh=mesh,
        in_specs=(
            P("tm", "mp"),
            P(),
            P(None, "mp"),
            P("mp", None),
            P(),
            P(None, None, "mp"),
            P("mp", None),
            P(None, "mp"),
            P("tm"),
            P("tm"),
        ),
        out_specs=P("tm", "mp"),
        check_vma=False,
    )
```
